32 devices in a mesh: groups: 1, pair: 32 (over z, y, x, core), coef: 1.
Axes of the slice: x: 2, y: 2, z: 4, core: 2. Of those that a mesh axis runs over, the one named last changes fastest.
Arguments:
- tiles: bfloat16 [256, 64, 64, 64], P(('pair', 'coef')), may hold values from -6 to 6
- occ_coef: bfloat16 [3968, 32], P('coef', 'groups'), may hold values from -0.75 to 0.75
- vir_coef: bfloat16 [3968, 3072], P('pair', 'coef'), may hold values from -0.09375 to 0.09375
- shell_pairs: int32 [2, 256], replicated, may hold values from 0 to 61
- live_flags: int32 [256], replicated, may hold values from 0 to 1, as said below
Outputs:
- mo_ints: bfloat16 [64, 32, 3072], P('pair', 'groups', 'coef')
The draws below stay inside these ranges and needn't reach their ends.
Inputs may be any that keep to these rules, and one draw needn't show every extreme that they name: `live_flags`: among the 8 slots of one device (aligned blocks of 8 entries) at least one and at most 4 flags are 1; some device has exactly 4.
All inputs are finite; a program needn't handle non-finite values.
Results may differ from the reference program's by a relative error of at most 0.0049.
Values may be sent and summed in bfloat16 or wider, within the bound.
No kernel may reach another device: no remote copies, remote signals or barrier semaphores. Data moves between devices by JAX's collectives and lax.ppermute only.
A program may use at most 128 MiB of HBM per device.

```python
import jax
import jax.numpy as jnp
from jax import lax

SH = 64
NAO = 3968
NOCC = 32
NVIR = 3072
LIVE = 4
NSH = 62
SLOTS = 8
KET = 64
BLOCKS = 256


def draw_live_flags(key, part):
    key = jax.random.fold_in(key, 3)
    device_count = BLOCKS // SLOTS
    key_count, key_full, key_rank = jax.random.split(key, 3)
    counts = jax.random.randint(key_count, (device_count,), 1, LIVE + 1)
    chosen = jax.random.randint(key_full, (), 0, device_count)
    counts = jnp.where(jnp.arange(device_count) == chosen, LIVE, counts)
    scores = jax.random.randint(key_rank, (device_count, SLOTS), 0, 2 ** 20) * SLOTS + jnp.arange(SLOTS)[None, :]
    ranks = jnp.argsort(jnp.argsort(scores, axis=1), axis=1)
    flags = (ranks < counts[:, None]).astype(jnp.int32)
    return flags.reshape(BLOCKS)


def place_ends(values, rng, low, largest):
    index_at = [jax.random.randint(jax.random.fold_in(rng, axis), (), 0, length) for axis, length in enumerate(values.shape)]
    widest = values.shape.index(max(values.shape))
    neighbour = index_at[:widest] + [(index_at[widest] + 1) % values.shape[widest]] + index_at[widest + 1:]
    return values.at[tuple(index_at)].set(low).at[tuple(neighbour)].set(largest)


def levels(rng, dims, cuts, low, high):
    gain, own = 1.0, jax.random.fold_in(rng, 6)
    for axis_at, parts in cuts:
        steps = jnp.exp(jax.random.uniform(jax.random.fold_in(own, axis_at), (parts,), jnp.float32, low / len(cuts), high / len(cuts)))
        gain = gain * jnp.repeat(steps, dims[axis_at] // parts).reshape([-1 if axis == axis_at else 1 for axis in range(len(dims))])
    return gain


def scatter_about(stream_key, dims, width, reach, cuts=(), kind=jnp.bfloat16):
    loudness = levels(stream_key, dims, cuts, -0.22, 0.18) if cuts else 1.0
    values = jax.random.normal(stream_key, dims, jnp.float32) * width * loudness
    return jnp.minimum(jnp.maximum(values, -reach), reach).astype(kind)


def setup_inputs(seed: int = 0, part: int = 0) -> dict:
    seeds = jax.random.split(jax.random.key(seed), 6)
    part_keys = jax.random.split(jax.random.fold_in(seeds[5], part), 6)
    tiles = scatter_about(seeds[0], (BLOCKS, SH, SH, KET), 1.0, 6.0, ((0, 32),))
    occ_coef = scatter_about(part_keys[1], (NAO, NOCC), 0.125, 0.75)
    vir_coef = scatter_about(seeds[2], (NAO, NVIR), NAO ** -0.5, 0.09375, ((0, 32),))
    shell_pairs = place_ends(jax.random.randint(seeds[3], (2, BLOCKS), 0, NSH), jax.random.fold_in(seeds[3], 1), 0, NSH - 1).astype(jnp.int32)
    live_flags = draw_live_flags(jax.random.fold_in(seeds[5], 71), part)
    return {"tiles": tiles, "occ_coef": occ_coef, "vir_coef": vir_coef, "shell_pairs": shell_pairs, "live_flags": live_flags}


def reference(tiles, occ_coef, vir_coef, shell_pairs, live_flags):
    shell_count = NAO // SH
    occ_shells = occ_coef.astype(jnp.float32).reshape(shell_count, SH, NOCC)

    def add_block(accum, items):
        tile_block, mu_shell, nu_shell, flag_value = items
        panel = occ_shells[mu_shell]
        contrib = jnp.einsum("mi,mnk->kin", panel, tile_block.astype(jnp.float32), precision=lax.Precision.HIGHEST)
        contrib = contrib * flag_value.astype(jnp.float32)
        return accum.at[nu_shell].add(contrib), None

    start_sum = jnp.zeros((shell_count, KET, NOCC, SH), jnp.float32)
    accum, unused = lax.scan(add_block, start_sum, (tiles, shell_pairs[0], shell_pairs[1], live_flags))
    half_ints = accum.transpose(1, 2, 0, 3).reshape(KET * NOCC, NAO).astype(jnp.bfloat16)
    result = jnp.dot(half_ints, vir_coef, preferred_element_type=jnp.float32)
    return result.reshape(KET, NOCC, NVIR).astype(jnp.bfloat16)
```

```python
import jax
import jax.numpy as jnp
from jax import lax
from jax.experimental import pallas as pl
from jax.experimental.pallas import tpu as pltpu
from jax.sharding import Mesh, PartitionSpec as P

LIVE = 4
FAR, NEAR, ROW, COL, CORE = "far", "near", "row", "col", "core"
AXES = (FAR, NEAR, ROW, COL, CORE)


def plain(tiles, occ_coef, vir_coef, shell_pairs, live_flags):
    slot_count, shell_size, unused_dim, ket_cols = tiles.shape
    pair_count = lax.axis_size("pair")
    coef_count = lax.axis_size("coef")
    core_index = lax.axis_index("coef")
    device_index = lax.axis_index(("pair", "coef"))
    occ_full = lax.all_gather(occ_coef, "coef", axis=0, tiled=True)
    basis_count, occ_count = occ_full.shape
    shell_count = basis_count // shell_size
    ket_owned = ket_cols // pair_count
    occ_shells = occ_full.reshape(shell_count, shell_size, occ_count)
    block_table = shell_pairs.reshape(2, pair_count * coef_count, slot_count)
    flag_table = live_flags.reshape(pair_count * coef_count, slot_count)
    own_mu = lax.dynamic_index_in_dim(block_table[0], device_index, 0, keepdims=False)
    own_flag = lax.dynamic_index_in_dim(flag_table, device_index, 0, keepdims=False)
    peer_nu = lax.dynamic_index_in_dim(
        block_table[1].reshape(pair_count, coef_count, slot_count), core_index, 1, keepdims=False
    )
    panels = jnp.take(occ_shells, own_mu, axis=0)
    result = jnp.einsum("bmi,bmnk->bkin", panels, tiles, preferred_element_type=jnp.float32)
    result = result * own_flag.astype(jnp.float32)[:, None, None, None]
    quarter = result.reshape(tiles.shape[0], ket_cols, occ_count * shell_size)
    received = lax.all_to_all(quarter, "pair", split_axis=1, concat_axis=0, tiled=True)
    recv_shells = peer_nu.reshape(-1)
    selector = (jnp.arange(shell_count, dtype=jnp.int32)[:, None] == recv_shells[None, :]).astype(
        jnp.float32
    )
    received = received.reshape(-1, ket_owned, occ_count, shell_size)
    partial_sum = jnp.einsum("gb,bkis->kigs", selector, received, precision=lax.Precision.HIGHEST)
    half_sum = lax.psum(partial_sum, "coef")
    half_ints = half_sum.reshape(ket_owned * occ_count, basis_count).astype(jnp.bfloat16)
    result = jnp.dot(
        half_ints,
        lax.all_gather(vir_coef, "pair", axis=0, tiled=True),
        preferred_element_type=jnp.float32,
    )
    return result.reshape(ket_owned, occ_count, vir_coef.shape[1]).astype(jnp.bfloat16)


def first_quarter_body(me_ref, flag_ref, pair_ref, occ_ref, tiles_ref, out_ref, held, turned, wide, sem, *, slots):
    live, shell_size, unused_dim, ket_cols = held.shape
    occ_count = occ_ref.shape[0]
    owners, groups, rows, lanes = out_ref.shape
    step = 16
    first = me_ref[0] * slots
    seen = jnp.int32(0)
    picks = [jnp.int32(0)] * live
    for slot in range(slots):
        flag = flag_ref[first + slot]
        picks = [jnp.where((flag == 1) & (seen == j), slot, pick) for j, pick in enumerate(picks)]
        seen = seen + flag
    copies = [
        pltpu.make_async_copy(tiles_ref.at[pick], held.at[j], sem.at[j]) for j, pick in enumerate(picks)
    ]
    for copy in copies:
        copy.start()
    inner = shell_size * step
    spread = (
        lax.broadcasted_iota(jnp.int32, (shell_size, inner), 1) // step
        == lax.broadcasted_iota(jnp.int32, (shell_size, inner), 0)
    ).astype(jnp.bfloat16)
    diagonal = lax.broadcasted_iota(jnp.int32, (step, inner), 1) % step == lax.broadcasted_iota(
        jnp.int32, (step, inner), 0
    )
    for j in range(live):
        mu = pair_ref[0, first + picks[j]]
        both = occ_ref[:, pl.ds(pl.multiple_of(lax.div(mu, 2) * 128, 128), 128)].astype(jnp.float32)
        both = jnp.where(lax.rem(mu, 2) == 1, pltpu.roll(both, shell_size, 1), both)
        panel = both[:, :shell_size].astype(jnp.bfloat16)
        panel = jnp.dot(panel, spread, preferred_element_type=jnp.float32)
        weight = jnp.where(diagonal[None], panel[:, None, :], 0.0).astype(jnp.bfloat16)
        weight = weight.reshape(occ_count * step, inner)
        copies[j].wait()
        for part in range(shell_size // step):
            block = held[j, :, part * step : (part + 1) * step, :].reshape(inner, ket_cols)
            result = jnp.dot(weight, block, preferred_element_type=jnp.float32)
            turned[j % 2, :, part * step : (part + 1) * step, :] = result.reshape(occ_count, step, ket_cols)
        if j % 2 == 1:
            for i in range(occ_count):
                value = turned[:, i].reshape(2 * shell_size, ket_cols)
                wide[pl.ds(i, ket_cols, stride=occ_count), :] = value.T
            out_ref[:, j // 2] = wide[...].astype(jnp.bfloat16).reshape(owners, rows, lanes)


def first_quarter(me, flags, pairs, occ, tiles, owners):
    slots, shell_size, unused_dim, ket_cols = tiles.shape
    occ_count = occ.shape[0]
    rows = ket_cols // owners * occ_count
    shape = (owners, LIVE // 2, rows, 2 * shell_size)

    def body(*refs):
        first_quarter_body(*refs, slots=slots)

    return pl.pallas_call(
        body,
        out_shape=jax.ShapeDtypeStruct(shape, jnp.bfloat16),
        in_specs=[pl.BlockSpec(memory_space=pltpu.SMEM)] * 3
        + [pl.BlockSpec(memory_space=pltpu.VMEM), pl.BlockSpec(memory_space=pl.ANY)],
        out_specs=pl.BlockSpec(memory_space=pltpu.VMEM),
        scratch_shapes=[
            pltpu.VMEM((LIVE, shell_size, shell_size, ket_cols), jnp.bfloat16),
            pltpu.VMEM((2, occ_count, shell_size, ket_cols), jnp.float32),
            pltpu.VMEM((ket_cols * occ_count, 2 * shell_size), jnp.float32),
            pltpu.SemaphoreType.DMA((LIVE,)),
        ],
        compiler_params=pltpu.CompilerParams(vmem_limit_bytes=32 * 1024 * 1024),
        cost_estimate=pl.CostEstimate(flops=10**9, bytes_accessed=6 * 10**6, transcendentals=0),
        name="first_quarter",
    )(me, flags, pairs, occ, tiles)


def sum_shells_body(nu_ref, at_ref, got_ref, out_ref, acc_ref, *, shell_size, depth, blocks):
    tile_count, rows, lanes = acc_ref.shape
    per = lanes // shell_size
    sources, groups = got_ref.shape[0], got_ref.shape[1]
    acc_ref[...] = jnp.zeros_like(acc_ref)
    lane = lax.broadcasted_iota(jnp.int32, (rows, lanes), 1)

    def add(source, carry):
        for group in range(groups):
            both = got_ref[source, group].astype(jnp.float32)
            turned = pltpu.roll(both, shell_size, 1)
            for part in range(per):
                shell = nu_ref[source * groups * per + group * per + part]
                place = lax.rem(shell, per)
                value = jnp.where(place == part, both, turned)
                value = jnp.where(lane // shell_size == place, value, 0.0)
                at = lax.div(shell, per)
                acc_ref[at] = acc_ref[at] + value
        return carry

    lax.fori_loop(0, sources, add, 0)
    far, col = at_ref[0], at_ref[1]
    for block in range(blocks):
        first = block * depth
        tile, shift = first // lanes, first % lanes
        turn = (lanes - shift) % lanes
        value = acc_ref[tile]
        if turn:
            value = pltpu.roll(value, turn, 1)
            if shift + depth > lanes:
                value = jnp.where(lane < turn, value, pltpu.roll(acc_ref[tile + 1], turn, 1))
        value = jnp.where(lane < depth, value, 0.0).astype(out_ref.dtype)
        bits = [(block >> b) & 1 for b in (4, 3, 2, 1, 0)]
        spot = 4 * jnp.bitwise_xor(far, bits[0]) + 2 * jnp.bitwise_xor(col, bits[3])
        for core in range(2):
            out_ref[4 * bits[1] + 2 * bits[2] + core, spot + (bits[4] ^ core)] = value


def sum_shells(nu, at, got, shell_size, shell_count, depth):
    sources, groups, rows, lanes = got.shape
    per = lanes // shell_size
    tile_count = shell_count // per + 1
    blocks = sources

    def body(*refs):
        sum_shells_body(*refs, shell_size=shell_size, depth=depth, blocks=blocks)

    return pl.pallas_call(
        body,
        out_shape=jax.ShapeDtypeStruct((8, blocks // 4, rows, lanes), jnp.bfloat16),
        in_specs=[
            pl.BlockSpec(memory_space=pltpu.SMEM),
            pl.BlockSpec(memory_space=pltpu.SMEM),
            pl.BlockSpec(memory_space=pltpu.VMEM),
        ],
        out_specs=pl.BlockSpec(memory_space=pltpu.VMEM),
        scratch_shapes=[pltpu.VMEM((tile_count, rows, lanes), jnp.float32)],
        compiler_params=pltpu.CompilerParams(vmem_limit_bytes=32 * 1024 * 1024),
        cost_estimate=pl.CostEstimate(flops=10**7, bytes_accessed=4 * 10**6, transcendentals=0),
        name="sum_shells",
    )(nu, at, got)


def transform_body(*refs, chunk):
    half_ref, out_ref = refs[0], refs[-1]
    panels = refs[1:-1]
    groups, blocks, rows, lanes = half_ref.shape
    depth, columns = panels[0].shape
    for start in range(0, columns, chunk):
        total = None
        for block, panel in enumerate(panels):
            half = half_ref[:, block].reshape(groups * rows, lanes)[:, :depth]
            term = jnp.dot(half, panel[:, start : start + chunk], preferred_element_type=jnp.float32)
            total = term if total is None else total + term
        out_ref[:, :, start : start + chunk] = total.astype(out_ref.dtype).reshape(groups, rows, chunk)


def transform(half, panels, chunk):
    groups, blocks, rows, lanes = half.shape
    depth, columns = panels[0].shape

    def body(*refs):
        transform_body(*refs, chunk=chunk)

    return pl.pallas_call(
        body,
        out_shape=jax.ShapeDtypeStruct((groups, rows, columns), jnp.bfloat16),
        in_specs=[pl.BlockSpec(memory_space=pltpu.VMEM)] * (1 + len(panels)),
        out_specs=pl.BlockSpec(memory_space=pltpu.VMEM),
        compiler_params=pltpu.CompilerParams(vmem_limit_bytes=32 * 1024 * 1024),
        cost_estimate=pl.CostEstimate(
            flops=2 * groups * rows * blocks * depth * columns, bytes_accessed=6 * 10**6, transcendentals=0
        ),
        name="second_quarter",
    )(half, *panels)


def on_device(tiles, occ_coef, vir_coef, shell_pairs, live_flags):
    slot_count, shell_size, unused_dim, ket_cols = tiles.shape
    basis_count, occ_count = occ_coef.shape
    shell_count = basis_count // shell_size
    depth, vir_count = vir_coef.shape
    device_count = lax.axis_size(AXES)
    device_index = lax.axis_index(AXES)
    core, far, col = lax.axis_index(CORE), lax.axis_index(FAR), lax.axis_index(COL)
    ket_owned = ket_cols // device_count
    swap = [(0, 1), (1, 0)]

    width = vir_count // 2
    keep = lax.dynamic_slice_in_dim(vir_coef, core * width, width, 1)
    give = lax.dynamic_slice_in_dim(vir_coef, (1 - core) * width, width, 1)
    near = [keep, lax.ppermute(give, CORE, swap)]
    beside = [lax.ppermute(panel, COL, swap) for panel in near]
    away = [lax.ppermute(panel, FAR, swap) for panel in near]

    flags = live_flags.reshape(device_count, slot_count)
    rank = jnp.cumsum(flags, axis=1) - 1
    chosen = (rank[:, None, :] == jnp.arange(LIVE)[None, :, None]) & (flags[:, None, :] == 1)
    nu_table = shell_pairs[1].reshape(device_count, 1, slot_count)
    nu = jnp.where(jnp.any(chosen, axis=2), jnp.sum(jnp.where(chosen, nu_table, 0), axis=2), shell_count)
    me = jnp.reshape(device_index, (1,)).astype(jnp.int32)
    quarter = first_quarter(me, live_flags, shell_pairs, occ_coef.T, tiles, device_count)
    quarter, near[1], beside[0], away[0] = lax.optimization_barrier((quarter, near[1], beside[0], away[0]))
    got = lax.all_to_all(quarter, AXES, split_axis=0, concat_axis=0, tiled=True)
    corner = [lax.ppermute(away[0], COL, swap)]
    got, beside[1], away[1], corner[0] = lax.optimization_barrier((got, beside[1], away[1], corner[0]))
    corner.append(lax.ppermute(away[1], COL, swap))

    half = sum_shells(nu.reshape(-1), jnp.stack([far, col]), got, shell_size, shell_count, depth)
    half = lax.all_to_all(half, (NEAR, ROW, CORE), split_axis=0, concat_axis=0, tiled=True)
    part = transform(half, near + beside + away + corner, 512)
    part = lax.all_to_all(part, (NEAR, ROW, CORE), split_axis=0, concat_axis=0, tiled=True)
    part = part.reshape(4, 2, ket_owned * occ_count, width).astype(jnp.float32).sum(axis=0)
    return part.transpose(1, 0, 2).reshape(ket_owned, occ_count, vir_count).astype(jnp.bfloat16)


def solution(mesh):
    shape = dict(mesh.shape)
    in_specs = (
        P(("pair", "coef"), None, None, None),
        P("coef", "groups"),
        P("pair", "coef"),
        P(),
        P(),
    )
    out_specs = P("pair", "groups", "coef")
    body = plain
    if shape["pair"] == 32 and shape["coef"] == 1 and shape["groups"] == 1:
        mesh = Mesh(mesh.devices.reshape(2, 2, 2, 2, 2), AXES)
        in_specs = (P(AXES), P(), P(AXES), P(), P())
        out_specs = P(AXES)
        body = on_device
    return jax.shard_map(body, mesh=mesh, in_specs=in_specs, out_specs=out_specs, check_vma=False)
```

```python
import jax
import jax.numpy as jnp
from jax import lax
from jax.experimental import pallas as pl
from jax.experimental.pallas import tpu as pltpu
from jax.sharding import Mesh, PartitionSpec as P

LIVE = 4
FAR, NEAR, ROW, COL, CORE = "far", "near", "row", "col", "core"
AXES = (FAR, NEAR, ROW, COL, CORE)


def plain(tiles, occ_coef, vir_coef, shell_pairs, live_flags):
    slot_count, shell_size, unused_dim, ket_cols = tiles.shape
    pair_count = lax.axis_size("pair")
    coef_count = lax.axis_size("coef")
    core_index = lax.axis_index("coef")
    device_index = lax.axis_index(("pair", "coef"))
    occ_full = lax.all_gather(occ_coef, "coef", axis=0, tiled=True)
    basis_count, occ_count = occ_full.shape
    shell_count = basis_count // shell_size
    ket_owned = ket_cols // pair_count
    occ_shells = occ_full.reshape(shell_count, shell_size, occ_count)
    block_table = shell_pairs.reshape(2, pair_count * coef_count, slot_count)
    flag_table = live_flags.reshape(pair_count * coef_count, slot_count)
    own_mu = lax.dynamic_index_in_dim(block_table[0], device_index, 0, keepdims=False)
    own_flag = lax.dynamic_index_in_dim(flag_table, device_index, 0, keepdims=False)
    peer_nu = lax.dynamic_index_in_dim(
        block_table[1].reshape(pair_count, coef_count, slot_count), core_index, 1, keepdims=False
    )
    panels = jnp.take(occ_shells, own_mu, axis=0)
    result = jnp.einsum("bmi,bmnk->bkin", panels, tiles, preferred_element_type=jnp.float32)
    result = result * own_flag.astype(jnp.float32)[:, None, None, None]
    quarter = result.reshape(tiles.shape[0], ket_cols, occ_count * shell_size)
    received = lax.all_to_all(quarter, "pair", split_axis=1, concat_axis=0, tiled=True)
    recv_shells = peer_nu.reshape(-1)
    selector = (jnp.arange(shell_count, dtype=jnp.int32)[:, None] == recv_shells[None, :]).astype(
        jnp.float32
    )
    received = received.reshape(-1, ket_owned, occ_count, shell_size)
    partial_sum = jnp.einsum("gb,bkis->kigs", selector, received, precision=lax.Precision.HIGHEST)
    half_sum = lax.psum(partial_sum, "coef")
    half_ints = half_sum.reshape(ket_owned * occ_count, basis_count).astype(jnp.bfloat16)
    result = jnp.dot(
        half_ints,
        lax.all_gather(vir_coef, "pair", axis=0, tiled=True),
        preferred_element_type=jnp.float32,
    )
    return result.reshape(ket_owned, occ_count, vir_coef.shape[1]).astype(jnp.bfloat16)


def shell_list_body(nu_ref, out_ref):
    out_ref[...] = nu_ref[...]


def shell_list(nu):
    return pl.pallas_call(
        shell_list_body,
        out_shape=jax.ShapeDtypeStruct(nu.shape, nu.dtype),
        in_specs=[pl.BlockSpec(memory_space=pltpu.VMEM)],
        out_specs=pl.BlockSpec(memory_space=pltpu.VMEM),
        cost_estimate=pl.CostEstimate(flops=10**11, bytes_accessed=10**6, transcendentals=0),
        name="shell_list",
    )(nu)


def first_quarter_body(me_ref, flag_ref, pair_ref, occ_ref, tiles_ref, out_ref, held, turned, wide, sem, *, slots):
    live, shell_size, unused_dim, ket_cols = held.shape
    occ_count = occ_ref.shape[0]
    owners, groups, rows, lanes = out_ref.shape
    step = 16
    first = me_ref[0] * slots
    seen = jnp.int32(0)
    picks = [jnp.int32(0)] * live
    for slot in range(slots):
        flag = flag_ref[first + slot]
        picks = [jnp.where((flag == 1) & (seen == j), slot, pick) for j, pick in enumerate(picks)]
        seen = seen + flag
    copies = [
        pltpu.make_async_copy(tiles_ref.at[pick], held.at[j], sem.at[j]) for j, pick in enumerate(picks)
    ]
    for copy in copies:
        copy.start()
    inner = shell_size * step
    spread = (
        lax.broadcasted_iota(jnp.int32, (shell_size, inner), 1) // step
        == lax.broadcasted_iota(jnp.int32, (shell_size, inner), 0)
    ).astype(jnp.bfloat16)
    diagonal = lax.broadcasted_iota(jnp.int32, (step, inner), 1) % step == lax.broadcasted_iota(
        jnp.int32, (step, inner), 0
    )
    for j in range(live):
        mu = pair_ref[0, first + picks[j]]
        both = occ_ref[:, pl.ds(pl.multiple_of(lax.div(mu, 2) * 128, 128), 128)].astype(jnp.float32)
        both = jnp.where(lax.rem(mu, 2) == 1, pltpu.roll(both, shell_size, 1), both)
        panel = both[:, :shell_size].astype(jnp.bfloat16)
        panel = jnp.dot(panel, spread, preferred_element_type=jnp.float32)
        weight = jnp.where(diagonal[None], panel[:, None, :], 0.0).astype(jnp.bfloat16)
        weight = weight.reshape(occ_count * step, inner)
        copies[j].wait()
        for part in range(shell_size // step):
            block = held[j, :, part * step : (part + 1) * step, :].reshape(inner, ket_cols)
            result = jnp.dot(weight, block, preferred_element_type=jnp.float32)
            turned[j % 2, :, part * step : (part + 1) * step, :] = result.reshape(occ_count, step, ket_cols)
        if j % 2 == 1:
            for i in range(occ_count):
                value = turned[:, i].reshape(2 * shell_size, ket_cols)
                wide[pl.ds(i, ket_cols, stride=occ_count), :] = value.T
            out_ref[:, j // 2] = wide[...].astype(jnp.bfloat16).reshape(owners, rows, lanes)


def first_quarter(me, flags, pairs, occ, tiles, owners):
    slots, shell_size, unused_dim, ket_cols = tiles.shape
    occ_count = occ.shape[0]
    rows = ket_cols // owners * occ_count
    shape = (owners, LIVE // 2, rows, 2 * shell_size)

    def body(*refs):
        first_quarter_body(*refs, slots=slots)

    return pl.pallas_call(
        body,
        out_shape=jax.ShapeDtypeStruct(shape, jnp.bfloat16),
        in_specs=[pl.BlockSpec(memory_space=pltpu.SMEM)] * 3
        + [pl.BlockSpec(memory_space=pltpu.VMEM), pl.BlockSpec(memory_space=pl.ANY)],
        out_specs=pl.BlockSpec(memory_space=pltpu.VMEM),
        scratch_shapes=[
            pltpu.VMEM((LIVE, shell_size, shell_size, ket_cols), jnp.bfloat16),
            pltpu.VMEM((2, occ_count, shell_size, ket_cols), jnp.float32),
            pltpu.VMEM((ket_cols * occ_count, 2 * shell_size), jnp.float32),
            pltpu.SemaphoreType.DMA((LIVE,)),
        ],
        compiler_params=pltpu.CompilerParams(vmem_limit_bytes=60 * 1024 * 1024),
        cost_estimate=pl.CostEstimate(flops=10**9, bytes_accessed=6 * 10**6, transcendentals=0),
        name="first_quarter",
    )(me, flags, pairs, occ, tiles)


def sum_shells_body(nu_ref, at_ref, got_ref, *refs, shell_size, depth):
    outs, acc_ref = refs[:-1], refs[-1]
    tile_count, rows, lanes = acc_ref.shape
    per = lanes // shell_size
    sources, groups = got_ref.shape[0], got_ref.shape[1]
    acc_ref[...] = jnp.zeros_like(acc_ref)
    lane = lax.broadcasted_iota(jnp.int32, (rows, lanes), 1)

    def add(source, carry):
        for group in range(groups):
            both = got_ref[source, group].astype(jnp.float32)
            turned = pltpu.roll(both, shell_size, 1)
            for part in range(per):
                shell = nu_ref[source * groups * per + group * per + part]
                place = lax.rem(shell, per)
                value = jnp.where(place == part, both, turned)
                value = jnp.where(lane // shell_size == place, value, 0.0)
                at = lax.div(shell, per)
                acc_ref[at] = acc_ref[at] + value
        return carry

    lax.fori_loop(0, sources, add, 0)
    step = lanes - depth
    for piece, out_ref in enumerate(outs):
        for spot in range(out_ref.shape[0]):
            flips = (piece >> 1, spot >> 2, (spot >> 1) & 1, spot & 1, piece & 1)
            block = jnp.int32(0)
            for axis, flip in enumerate(flips):
                block = 2 * block + jnp.bitwise_xor(at_ref[axis], flip)
            turn = block * step
            before = pltpu.roll(acc_ref[jnp.maximum(block - 1, 0)], turn, 1)
            after = pltpu.roll(acc_ref[block], turn, 1)
            value = jnp.where(lane < turn, before, after)
            out_ref[spot] = jnp.where(lane < depth, value, 0.0).astype(out_ref.dtype)


def sum_shells(nu, at, got, shell_size, shell_count, depth):
    sources, groups, rows, lanes = got.shape
    tile_count = shell_count // (lanes // shell_size) + 1

    def body(*refs):
        sum_shells_body(*refs, shell_size=shell_size, depth=depth)

    return pl.pallas_call(
        body,
        out_shape=[jax.ShapeDtypeStruct((sources // 4, rows, lanes), jnp.bfloat16)] * 4,
        in_specs=[
            pl.BlockSpec(memory_space=pltpu.SMEM),
            pl.BlockSpec(memory_space=pltpu.SMEM),
            pl.BlockSpec(memory_space=pltpu.VMEM),
        ],
        out_specs=[pl.BlockSpec(memory_space=pltpu.VMEM)] * 4,
        scratch_shapes=[pltpu.VMEM((tile_count, rows, lanes), jnp.float32)],
        compiler_params=pltpu.CompilerParams(vmem_limit_bytes=32 * 1024 * 1024),
        cost_estimate=pl.CostEstimate(flops=10**7, bytes_accessed=4 * 10**6, transcendentals=0),
        name="sum_shells",
    )(nu, at, got)


def transform_body(*refs, chunk, part, count, pieces):
    halves, panels = refs[:pieces], refs[pieces : pieces + count]
    outs, held, sems = refs[pieces + count : -2], refs[-2], refs[-1]
    depth, columns = panels[0].shape
    rows = halves[0].shape[1]
    copies = [
        [
            pltpu.make_async_copy(panel.at[:, pl.ds(start, chunk)], held.at[block, :, pl.ds(start, chunk)], sems.at[step, block])
            for block, panel in enumerate(panels)
        ]
        for step, start in enumerate(range(0, columns, chunk))
    ]
    for row in copies:
        for copy in row:
            copy.start()
    for start in range(0, columns, part):
        total = None
        for block in range(count):
            if start % chunk == 0:
                copies[start // chunk][block].wait()
            half = jnp.concatenate([half_ref[block] for half_ref in halves], axis=0)[:, :depth]
            term = jnp.dot(half, held[block, :, start : start + part], preferred_element_type=jnp.float32)
            total = term if total is None else total + term
        for piece, out_ref in enumerate(outs):
            out_ref[:, start : start + part] = total[piece * rows : (piece + 1) * rows].astype(out_ref.dtype)


def transform(halves, panels, dtypes, chunk, part):
    blocks, rows, lanes = halves[0].shape
    depth, columns = panels[0].shape
    pieces = len(halves)

    def body(*refs):
        transform_body(*refs, chunk=chunk, part=part, count=blocks, pieces=pieces)

    return pl.pallas_call(
        body,
        out_shape=[jax.ShapeDtypeStruct((rows, columns), dtype) for dtype in dtypes],
        in_specs=[pl.BlockSpec(memory_space=pltpu.VMEM)] * pieces + [pl.BlockSpec(memory_space=pl.ANY)] * blocks,
        out_specs=[pl.BlockSpec(memory_space=pltpu.VMEM)] * pieces,
        scratch_shapes=[
            pltpu.VMEM((blocks, depth, columns), jnp.bfloat16),
            pltpu.SemaphoreType.DMA((columns // chunk, blocks)),
        ],
        compiler_params=pltpu.CompilerParams(vmem_limit_bytes=60 * 1024 * 1024),
        cost_estimate=pl.CostEstimate(
            flops=2 * pieces * rows * blocks * depth * columns, bytes_accessed=8 * 10**6, transcendentals=0
        ),
        name="second_quarter",
    )(*halves, *panels)


def on_device(tiles, occ_coef, vir_coef, shell_pairs, live_flags):
    slot_count, shell_size, unused_dim, ket_cols = tiles.shape
    basis_count, occ_count = occ_coef.shape
    shell_count = basis_count // shell_size
    depth, vir_count = vir_coef.shape
    device_count = lax.axis_size(AXES)
    device_index = lax.axis_index(AXES)
    ket_owned = ket_cols // device_count
    swap = [(0, 1), (1, 0)]

    diagonal = [(i, 3 - i) for i in range(4)]
    by_near = lax.ppermute(vir_coef, NEAR, swap)
    by_row = lax.ppermute(vir_coef, ROW, swap)
    by_col = lax.ppermute(vir_coef, COL, swap)

    flags = live_flags.reshape(device_count, slot_count)
    rank = jnp.cumsum(flags, axis=1) - 1
    chosen = (rank[:, None, :] == jnp.arange(LIVE)[None, :, None]) & (flags[:, None, :] == 1)
    nu_table = shell_pairs[1].reshape(device_count, 1, slot_count)
    nu = jnp.where(jnp.any(chosen, axis=2), jnp.sum(jnp.where(chosen, nu_table, 0), axis=2), shell_count)
    me = jnp.reshape(device_index, (1,)).astype(jnp.int32)
    quarter = first_quarter(me, live_flags, shell_pairs, occ_coef.T, tiles, device_count)
    quarter, by_near, by_row, by_col = lax.optimization_barrier((quarter, by_near, by_row, by_col))
    got = lax.all_to_all(quarter, AXES, split_axis=0, concat_axis=0, tiled=True)
    near_row = lax.ppermute(by_near, ROW, swap)
    near_col = lax.ppermute(by_col, NEAR, swap)
    row_col = lax.ppermute(by_row, COL, swap)

    at = jnp.stack([lax.axis_index(axis) for axis in AXES])
    own, to_core, to_far, to_both = sum_shells(nu.reshape(-1), at, got, shell_size, shell_count, depth)
    own, near_row = lax.optimization_barrier((own, near_row))
    all_three = lax.ppermute(near_row, COL, swap)
    panels = [vir_coef, by_col, by_row, row_col, by_near, near_col, near_row, all_three]
    from_far = lax.ppermute(to_far, FAR, swap)
    from_both = lax.ppermute(to_both, (FAR, CORE), diagonal)
    from_core = lax.ppermute(to_core, CORE, swap)
    wide, narrow = jnp.float32, jnp.bfloat16
    own_part, own_peer, far_part, far_peer = transform(
        [own, from_core, from_far, from_both], panels, [wide, narrow, wide, narrow], 1024, 512
    )
    far_peer = lax.ppermute(far_peer, CORE, swap)
    far_part = (far_part + far_peer.astype(jnp.float32)).astype(jnp.bfloat16)
    own_peer, far_part = lax.optimization_barrier((own_peer, far_part))
    taken = lax.ppermute(far_part, FAR, swap)
    own_peer = lax.ppermute(own_peer, CORE, swap)
    total = own_part + own_peer.astype(jnp.float32) + taken.astype(jnp.float32)
    return total.reshape(ket_owned, occ_count, vir_count).astype(jnp.bfloat16)


def solution(mesh):
    shape = dict(mesh.shape)
    in_specs = (
        P(("pair", "coef"), None, None, None),
        P("coef", "groups"),
        P("pair", "coef"),
        P(),
        P(),
    )
    out_specs = P("pair", "groups", "coef")
    body = plain
    if shape["pair"] == 32 and shape["coef"] == 1 and shape["groups"] == 1:
        mesh = Mesh(mesh.devices.reshape(2, 2, 2, 2, 2), AXES)
        in_specs = (P(AXES), P(), P(AXES), P(), P())
        out_specs = P(AXES)
        body = on_device
    return jax.shard_map(body, mesh=mesh, in_specs=in_specs, out_specs=out_specs, check_vma=False)
```

```python
import jax
import jax.numpy as jnp
from jax import lax
from jax.experimental import pallas as pl
from jax.experimental.pallas import tpu as pltpu
from jax.sharding import Mesh, PartitionSpec as P

LIVE = 4
FAR, NEAR, ROW, COL, CORE = "far", "near", "row", "col", "core"
AXES = (FAR, NEAR, ROW, COL, CORE)


def plain(tiles, occ_coef, vir_coef, shell_pairs, live_flags):
    slot_count, shell_size, unused_dim, ket_cols = tiles.shape
    pair_count = lax.axis_size("pair")
    coef_count = lax.axis_size("coef")
    core_index = lax.axis_index("coef")
    device_index = lax.axis_index(("pair", "coef"))
    occ_full = lax.all_gather(occ_coef, "coef", axis=0, tiled=True)
    basis_count, occ_count = occ_full.shape
    shell_count = basis_count // shell_size
    ket_owned = ket_cols // pair_count
    occ_shells = occ_full.reshape(shell_count, shell_size, occ_count)
    block_table = shell_pairs.reshape(2, pair_count * coef_count, slot_count)
    flag_table = live_flags.reshape(pair_count * coef_count, slot_count)
    own_mu = lax.dynamic_index_in_dim(block_table[0], device_index, 0, keepdims=False)
    own_flag = lax.dynamic_index_in_dim(flag_table, device_index, 0, keepdims=False)
    peer_nu = lax.dynamic_index_in_dim(
        block_table[1].reshape(pair_count, coef_count, slot_count), core_index, 1, keepdims=False
    )
    panels = jnp.take(occ_shells, own_mu, axis=0)
    result = jnp.einsum("bmi,bmnk->bkin", panels, tiles, preferred_element_type=jnp.float32)
    result = result * own_flag.astype(jnp.float32)[:, None, None, None]
    quarter = result.reshape(tiles.shape[0], ket_cols, occ_count * shell_size)
    received = lax.all_to_all(quarter, "pair", split_axis=1, concat_axis=0, tiled=True)
    recv_shells = peer_nu.reshape(-1)
    selector = (jnp.arange(shell_count, dtype=jnp.int32)[:, None] == recv_shells[None, :]).astype(
        jnp.float32
    )
    received = received.reshape(-1, ket_owned, occ_count, shell_size)
    partial_sum = jnp.einsum("gb,bkis->kigs", selector, received, precision=lax.Precision.HIGHEST)
    half_sum = lax.psum(partial_sum, "coef")
    half_ints = half_sum.reshape(ket_owned * occ_count, basis_count).astype(jnp.bfloat16)
    result = jnp.dot(
        half_ints,
        lax.all_gather(vir_coef, "pair", axis=0, tiled=True),
        preferred_element_type=jnp.float32,
    )
    return result.reshape(ket_owned, occ_count, vir_coef.shape[1]).astype(jnp.bfloat16)


def shell_list_body(nu_ref, out_ref):
    out_ref[...] = nu_ref[...]


def shell_list(nu):
    return pl.pallas_call(
        shell_list_body,
        out_shape=jax.ShapeDtypeStruct(nu.shape, nu.dtype),
        in_specs=[pl.BlockSpec(memory_space=pltpu.VMEM)],
        out_specs=pl.BlockSpec(memory_space=pltpu.VMEM),
        cost_estimate=pl.CostEstimate(flops=10**11, bytes_accessed=10**6, transcendentals=0),
        name="shell_list",
    )(nu)


def first_quarter_body(me_ref, flag_ref, pair_ref, occ_ref, tiles_ref, out_ref, held, turned, wide, sem, *, slots):
    live, shell_size, unused_dim, ket_cols = held.shape
    occ_count = occ_ref.shape[0]
    owners, groups, rows, lanes = out_ref.shape
    step = 16
    first = me_ref[0] * slots
    seen = jnp.int32(0)
    picks = [jnp.int32(0)] * live
    for slot in range(slots):
        flag = flag_ref[first + slot]
        picks = [jnp.where((flag == 1) & (seen == j), slot, pick) for j, pick in enumerate(picks)]
        seen = seen + flag
    copies = [
        pltpu.make_async_copy(tiles_ref.at[pick], held.at[j], sem.at[j]) for j, pick in enumerate(picks)
    ]
    for copy in copies:
        copy.start()
    inner = shell_size * step
    spread = (
        lax.broadcasted_iota(jnp.int32, (shell_size, inner), 1) // step
        == lax.broadcasted_iota(jnp.int32, (shell_size, inner), 0)
    ).astype(jnp.bfloat16)
    diagonal = lax.broadcasted_iota(jnp.int32, (step, inner), 1) % step == lax.broadcasted_iota(
        jnp.int32, (step, inner), 0
    )
    for j in range(live):
        mu = pair_ref[0, first + picks[j]]
        both = occ_ref[:, pl.ds(pl.multiple_of(lax.div(mu, 2) * 128, 128), 128)].astype(jnp.float32)
        both = jnp.where(lax.rem(mu, 2) == 1, pltpu.roll(both, shell_size, 1), both)
        panel = both[:, :shell_size].astype(jnp.bfloat16)
        panel = jnp.dot(panel, spread, preferred_element_type=jnp.float32)
        weight = jnp.where(diagonal[None], panel[:, None, :], 0.0).astype(jnp.bfloat16)
        weight = weight.reshape(occ_count * step, inner)
        copies[j].wait()
        for part in range(shell_size // step):
            block = held[j, :, part * step : (part + 1) * step, :].reshape(inner, ket_cols)
            result = jnp.dot(weight, block, preferred_element_type=jnp.float32)
            turned[j % 2, :, part * step : (part + 1) * step, :] = result.reshape(occ_count, step, ket_cols)
        if j % 2 == 1:
            for i in range(occ_count):
                value = turned[:, i].reshape(2 * shell_size, ket_cols)
                wide[pl.ds(i, ket_cols, stride=occ_count), :] = value.T
            out_ref[:, j // 2] = wide[...].astype(jnp.bfloat16).reshape(owners, rows, lanes)


def first_quarter(me, flags, pairs, occ, tiles, owners):
    slots, shell_size, unused_dim, ket_cols = tiles.shape
    occ_count = occ.shape[0]
    rows = ket_cols // owners * occ_count
    shape = (owners, LIVE // 2, rows, 2 * shell_size)

    def body(*refs):
        first_quarter_body(*refs, slots=slots)

    return pl.pallas_call(
        body,
        out_shape=jax.ShapeDtypeStruct(shape, jnp.bfloat16),
        in_specs=[pl.BlockSpec(memory_space=pltpu.SMEM)] * 3
        + [pl.BlockSpec(memory_space=pltpu.VMEM), pl.BlockSpec(memory_space=pl.ANY)],
        out_specs=pl.BlockSpec(memory_space=pltpu.VMEM),
        scratch_shapes=[
            pltpu.VMEM((LIVE, shell_size, shell_size, ket_cols), jnp.bfloat16),
            pltpu.VMEM((2, occ_count, shell_size, ket_cols), jnp.float32),
            pltpu.VMEM((ket_cols * occ_count, 2 * shell_size), jnp.float32),
            pltpu.SemaphoreType.DMA((LIVE,)),
        ],
        compiler_params=pltpu.CompilerParams(vmem_limit_bytes=60 * 1024 * 1024),
        cost_estimate=pl.CostEstimate(flops=10**9, bytes_accessed=6 * 10**6, transcendentals=0),
        name="first_quarter",
    )(me, flags, pairs, occ, tiles)


def sum_shells_body(nu_ref, at_ref, got_ref, *refs, shell_size, depth):
    outs, acc_ref = refs[:-1], refs[-1]
    tile_count, rows, lanes = acc_ref.shape
    per = lanes // shell_size
    sources, groups = got_ref.shape[0], got_ref.shape[1]
    acc_ref[...] = jnp.zeros_like(acc_ref)
    lane = lax.broadcasted_iota(jnp.int32, (rows, lanes), 1)

    def add(source, carry):
        for group in range(groups):
            both = got_ref[source, group].astype(jnp.float32)
            turned = pltpu.roll(both, shell_size, 1)
            for part in range(per):
                shell = nu_ref[source * groups * per + group * per + part]
                place = lax.rem(shell, per)
                value = jnp.where(place == part, both, turned)
                value = jnp.where(lane // shell_size == place, value, 0.0)
                at = lax.div(shell, per)
                acc_ref[at] = acc_ref[at] + value
        return carry

    lax.fori_loop(0, sources, add, 0)
    step = lanes - depth
    for piece, out_ref in enumerate(outs):
        for spot in range(out_ref.shape[0]):
            flips = (piece >> 1, spot >> 2, (spot >> 1) & 1, spot & 1, piece & 1)
            block = jnp.int32(0)
            for axis, flip in enumerate(flips):
                block = 2 * block + jnp.bitwise_xor(at_ref[axis], flip)
            turn = block * step
            before = pltpu.roll(acc_ref[jnp.maximum(block - 1, 0)], turn, 1)
            after = pltpu.roll(acc_ref[block], turn, 1)
            value = jnp.where(lane < turn, before, after)
            out_ref[spot] = jnp.where(lane < depth, value, 0.0).astype(out_ref.dtype)


def sum_shells(nu, at, got, shell_size, shell_count, depth):
    sources, groups, rows, lanes = got.shape
    tile_count = shell_count // (lanes // shell_size) + 1

    def body(*refs):
        sum_shells_body(*refs, shell_size=shell_size, depth=depth)

    return pl.pallas_call(
        body,
        out_shape=[jax.ShapeDtypeStruct((sources // 4, rows, lanes), jnp.bfloat16)] * 4,
        in_specs=[
            pl.BlockSpec(memory_space=pltpu.SMEM),
            pl.BlockSpec(memory_space=pltpu.SMEM),
            pl.BlockSpec(memory_space=pltpu.VMEM),
        ],
        out_specs=[pl.BlockSpec(memory_space=pltpu.VMEM)] * 4,
        scratch_shapes=[pltpu.VMEM((tile_count, rows, lanes), jnp.float32)],
        compiler_params=pltpu.CompilerParams(vmem_limit_bytes=32 * 1024 * 1024),
        cost_estimate=pl.CostEstimate(flops=10**7, bytes_accessed=4 * 10**6, transcendentals=0),
        name="sum_shells",
    )(nu, at, got)


def transform_body(*refs, chunk, part, count, pieces):
    halves, panels = refs[:pieces], refs[pieces : pieces + count]
    outs, held, sems = refs[pieces + count : -2], refs[-2], refs[-1]
    depth, columns = panels[0].shape
    rows = halves[0].shape[1]
    copies = [
        [
            pltpu.make_async_copy(panel.at[:, pl.ds(start, chunk)], held.at[block, :, pl.ds(start, chunk)], sems.at[step, block])
            for block, panel in enumerate(panels)
        ]
        for step, start in enumerate(range(0, columns, chunk))
    ]
    for row in copies:
        for copy in row:
            copy.start()
    for start in range(0, columns, part):
        total = None
        for block in range(count):
            if start % chunk == 0:
                copies[start // chunk][block].wait()
            half = jnp.concatenate([half_ref[block] for half_ref in halves], axis=0)[:, :depth]
            term = jnp.dot(half, held[block, :, start : start + part], preferred_element_type=jnp.float32)
            total = term if total is None else total + term
        for piece, out_ref in enumerate(outs):
            out_ref[:, start : start + part] = total[piece * rows : (piece + 1) * rows].astype(out_ref.dtype)


def transform(halves, panels, dtypes, chunk, part):
    blocks, rows, lanes = halves[0].shape
    depth, columns = panels[0].shape
    pieces = len(halves)

    def body(*refs):
        transform_body(*refs, chunk=chunk, part=part, count=blocks, pieces=pieces)

    return pl.pallas_call(
        body,
        out_shape=[jax.ShapeDtypeStruct((rows, columns), dtype) for dtype in dtypes],
        in_specs=[pl.BlockSpec(memory_space=pltpu.VMEM)] * pieces + [pl.BlockSpec(memory_space=pl.ANY)] * blocks,
        out_specs=[pl.BlockSpec(memory_space=pltpu.VMEM)] * pieces,
        scratch_shapes=[
            pltpu.VMEM((blocks, depth, columns), jnp.bfloat16),
            pltpu.SemaphoreType.DMA((columns // chunk, blocks)),
        ],
        compiler_params=pltpu.CompilerParams(vmem_limit_bytes=60 * 1024 * 1024),
        cost_estimate=pl.CostEstimate(
            flops=2 * pieces * rows * blocks * depth * columns, bytes_accessed=8 * 10**6, transcendentals=0
        ),
        name="second_quarter",
    )(*halves, *panels)


def on_device(tiles, occ_coef, vir_coef, shell_pairs, live_flags):
    slot_count, shell_size, unused_dim, ket_cols = tiles.shape
    basis_count, occ_count = occ_coef.shape
    shell_count = basis_count // shell_size
    depth, vir_count = vir_coef.shape
    device_count = lax.axis_size(AXES)
    device_index = lax.axis_index(AXES)
    ket_owned = ket_cols // device_count
    swap = [(0, 1), (1, 0)]

    diagonal = [(i, 3 - i) for i in range(4)]
    by_near = lax.ppermute(vir_coef, NEAR, swap)
    by_row = lax.ppermute(vir_coef, ROW, swap)
    by_col = lax.ppermute(vir_coef, COL, swap)

    flags = live_flags.reshape(device_count, slot_count)
    rank = jnp.cumsum(flags, axis=1) - 1
    chosen = (rank[:, None, :] == jnp.arange(LIVE)[None, :, None]) & (flags[:, None, :] == 1)
    nu_table = shell_pairs[1].reshape(device_count, 1, slot_count)
    nu = jnp.where(jnp.any(chosen, axis=2), jnp.sum(jnp.where(chosen, nu_table, 0), axis=2), shell_count)
    me = jnp.reshape(device_index, (1,)).astype(jnp.int32)
    quarter = first_quarter(me, live_flags, shell_pairs, occ_coef.T, tiles, device_count)
    got = lax.all_to_all(quarter, AXES, split_axis=0, concat_axis=0, tiled=True)
    near_row = lax.ppermute(by_near, ROW, swap)
    near_col = lax.ppermute(by_col, NEAR, swap)
    row_col = lax.ppermute(by_row, COL, swap)

    at = jnp.stack([lax.axis_index(axis) for axis in AXES])
    own, to_core, to_far, to_both = sum_shells(shell_list(nu).reshape(-1), at, got, shell_size, shell_count, depth)
    own, near_row = lax.optimization_barrier((own, near_row))
    all_three = lax.ppermute(near_row, COL, swap)
    panels = [vir_coef, by_col, by_row, row_col, by_near, near_col, near_row, all_three]
    from_far = lax.ppermute(to_far, FAR, swap)
    from_both = lax.ppermute(to_both, (FAR, CORE), diagonal)
    from_core = lax.ppermute(to_core, CORE, swap)
    wide, narrow = jnp.float32, jnp.bfloat16
    own_part, own_peer, far_part, far_peer = transform(
        [own, from_core, from_far, from_both], panels, [wide, narrow, wide, narrow], 1024, 512
    )
    far_peer = lax.ppermute(far_peer, CORE, swap)
    far_part = (far_part + far_peer.astype(jnp.float32)).astype(jnp.bfloat16)
    own_peer, far_part = lax.optimization_barrier((own_peer, far_part))
    taken = lax.ppermute(far_part, FAR, swap)
    own_peer = lax.ppermute(own_peer, CORE, swap)
    total = own_part + own_peer.astype(jnp.float32) + taken.astype(jnp.float32)
    return total.reshape(ket_owned, occ_count, vir_count).astype(jnp.bfloat16)


def solution(mesh):
    shape = dict(mesh.shape)
    in_specs = (
        P(("pair", "coef"), None, None, None),
        P("coef", "groups"),
        P("pair", "coef"),
        P(),
        P(),
    )
    out_specs = P("pair", "groups", "coef")
    body = plain
    if shape["pair"] == 32 and shape["coef"] == 1 and shape["groups"] == 1:
        mesh = Mesh(mesh.devices.reshape(2, 2, 2, 2, 2), AXES)
        in_specs = (P(AXES), P(), P(AXES), P(), P())
        out_specs = P(AXES)
        body = on_device
    return jax.shard_map(body, mesh=mesh, in_specs=in_specs, out_specs=out_specs, check_vma=False)
```

```python
import jax
import jax.numpy as jnp
from jax import lax
from jax.experimental import pallas as pl
from jax.experimental.pallas import tpu as pltpu
from jax.sharding import Mesh, PartitionSpec as P

LIVE = 4
FAR, NEAR, ROW, COL, CORE = "far", "near", "row", "col", "core"
AXES = (FAR, NEAR, ROW, COL, CORE)


def plain(tiles, occ_coef, vir_coef, shell_pairs, live_flags):
    slot_count, shell_size, unused_dim, ket_cols = tiles.shape
    pair_count = lax.axis_size("pair")
    coef_count = lax.axis_size("coef")
    core_index = lax.axis_index("coef")
    device_index = lax.axis_index(("pair", "coef"))
    occ_full = lax.all_gather(occ_coef, "coef", axis=0, tiled=True)
    basis_count, occ_count = occ_full.shape
    shell_count = basis_count // shell_size
    ket_owned = ket_cols // pair_count
    occ_shells = occ_full.reshape(shell_count, shell_size, occ_count)
    block_table = shell_pairs.reshape(2, pair_count * coef_count, slot_count)
    flag_table = live_flags.reshape(pair_count * coef_count, slot_count)
    own_mu = lax.dynamic_index_in_dim(block_table[0], device_index, 0, keepdims=False)
    own_flag = lax.dynamic_index_in_dim(flag_table, device_index, 0, keepdims=False)
    peer_nu = lax.dynamic_index_in_dim(
        block_table[1].reshape(pair_count, coef_count, slot_count), core_index, 1, keepdims=False
    )
    panels = jnp.take(occ_shells, own_mu, axis=0)
    result = jnp.einsum("bmi,bmnk->bkin", panels, tiles, preferred_element_type=jnp.float32)
    result = result * own_flag.astype(jnp.float32)[:, None, None, None]
    quarter = result.reshape(tiles.shape[0], ket_cols, occ_count * shell_size)
    received = lax.all_to_all(quarter, "pair", split_axis=1, concat_axis=0, tiled=True)
    recv_shells = peer_nu.reshape(-1)
    selector = (jnp.arange(shell_count, dtype=jnp.int32)[:, None] == recv_shells[None, :]).astype(
        jnp.float32
    )
    received = received.reshape(-1, ket_owned, occ_count, shell_size)
    partial_sum = jnp.einsum("gb,bkis->kigs", selector, received, precision=lax.Precision.HIGHEST)
    half_sum = lax.psum(partial_sum, "coef")
    half_ints = half_sum.reshape(ket_owned * occ_count, basis_count).astype(jnp.bfloat16)
    result = jnp.dot(
        half_ints,
        lax.all_gather(vir_coef, "pair", axis=0, tiled=True),
        preferred_element_type=jnp.float32,
    )
    return result.reshape(ket_owned, occ_count, vir_coef.shape[1]).astype(jnp.bfloat16)


def shell_list_body(nu_ref, out_ref):
    out_ref[...] = nu_ref[...]


def shell_list(nu):
    return pl.pallas_call(
        shell_list_body,
        out_shape=jax.ShapeDtypeStruct(nu.shape, nu.dtype),
        in_specs=[pl.BlockSpec(memory_space=pltpu.VMEM)],
        out_specs=pl.BlockSpec(memory_space=pltpu.VMEM),
        cost_estimate=pl.CostEstimate(flops=10**11, bytes_accessed=10**6, transcendentals=0),
        name="shell_list",
    )(nu)


def first_quarter_body(me_ref, flag_ref, pair_ref, occ_ref, tiles_ref, out_ref, held, turned, wide, sem, *, slots):
    live, shell_size, unused_dim, ket_cols = held.shape
    occ_count = occ_ref.shape[0]
    owners, groups, rows, lanes = out_ref.shape
    step = 16
    first = me_ref[0] * slots
    seen = jnp.int32(0)
    picks = [jnp.int32(0)] * live
    for slot in range(slots):
        flag = flag_ref[first + slot]
        picks = [jnp.where((flag == 1) & (seen == j), slot, pick) for j, pick in enumerate(picks)]
        seen = seen + flag
    copies = [
        pltpu.make_async_copy(tiles_ref.at[pick], held.at[j], sem.at[j]) for j, pick in enumerate(picks)
    ]
    for copy in copies:
        copy.start()
    inner = shell_size * step
    spread = (
        lax.broadcasted_iota(jnp.int32, (shell_size, inner), 1) // step
        == lax.broadcasted_iota(jnp.int32, (shell_size, inner), 0)
    ).astype(jnp.bfloat16)
    diagonal = lax.broadcasted_iota(jnp.int32, (step, inner), 1) % step == lax.broadcasted_iota(
        jnp.int32, (step, inner), 0
    )
    for j in range(live):
        mu = pair_ref[0, first + picks[j]]
        both = occ_ref[:, pl.ds(pl.multiple_of(lax.div(mu, 2) * 128, 128), 128)].astype(jnp.float32)
        both = jnp.where(lax.rem(mu, 2) == 1, pltpu.roll(both, shell_size, 1), both)
        panel = both[:, :shell_size].astype(jnp.bfloat16)
        panel = jnp.dot(panel, spread, preferred_element_type=jnp.float32)
        weight = jnp.where(diagonal[None], panel[:, None, :], 0.0).astype(jnp.bfloat16)
        weight = weight.reshape(occ_count * step, inner)
        copies[j].wait()
        for part in range(0, shell_size // step, 2):
            block = jnp.concatenate(
                [held[j, :, p * step : (p + 1) * step, :].reshape(inner, ket_cols) for p in (part, part + 1)], axis=1
            )
            result = jnp.dot(weight, block, preferred_element_type=jnp.float32)
            for p in range(2):
                at = (part + p) * step
                turned[j % 2, :, at : at + step, :] = result[:, p * ket_cols : (p + 1) * ket_cols].reshape(
                    occ_count, step, ket_cols
                )
        if j % 2 == 1:
            for i in range(occ_count):
                value = turned[:, i].reshape(2 * shell_size, ket_cols)
                wide[pl.ds(i, ket_cols, stride=occ_count), :] = value.T
            out_ref[:, j // 2] = wide[...].astype(jnp.bfloat16).reshape(owners, rows, lanes)


def first_quarter(me, flags, pairs, occ, tiles, owners):
    slots, shell_size, unused_dim, ket_cols = tiles.shape
    occ_count = occ.shape[0]
    rows = ket_cols // owners * occ_count
    shape = (owners, LIVE // 2, rows, 2 * shell_size)

    def body(*refs):
        first_quarter_body(*refs, slots=slots)

    return pl.pallas_call(
        body,
        out_shape=jax.ShapeDtypeStruct(shape, jnp.bfloat16),
        in_specs=[pl.BlockSpec(memory_space=pltpu.SMEM)] * 3
        + [pl.BlockSpec(memory_space=pltpu.VMEM), pl.BlockSpec(memory_space=pl.ANY)],
        out_specs=pl.BlockSpec(memory_space=pltpu.VMEM),
        scratch_shapes=[
            pltpu.VMEM((LIVE, shell_size, shell_size, ket_cols), jnp.bfloat16),
            pltpu.VMEM((2, occ_count, shell_size, ket_cols), jnp.float32),
            pltpu.VMEM((ket_cols * occ_count, 2 * shell_size), jnp.float32),
            pltpu.SemaphoreType.DMA((LIVE,)),
        ],
        compiler_params=pltpu.CompilerParams(vmem_limit_bytes=60 * 1024 * 1024),
        cost_estimate=pl.CostEstimate(flops=10**9, bytes_accessed=6 * 10**6, transcendentals=0),
        name="first_quarter",
    )(me, flags, pairs, occ, tiles)


def sum_shells_body(nu_ref, at_ref, got_ref, *refs, shell_size, depth):
    outs, acc_ref = refs[:-1], refs[-1]
    tile_count, rows, lanes = acc_ref.shape
    per = lanes // shell_size
    sources, groups = got_ref.shape[0], got_ref.shape[1]
    acc_ref[...] = jnp.zeros_like(acc_ref)
    lane = lax.broadcasted_iota(jnp.int32, (rows, lanes), 1)

    def add(source, carry):
        for group in range(groups):
            both = got_ref[source, group].astype(jnp.float32)
            turned = pltpu.roll(both, shell_size, 1)
            for part in range(per):
                shell = nu_ref[source * groups * per + group * per + part]
                place = lax.rem(shell, per)
                value = jnp.where(place == part, both, turned)
                value = jnp.where(lane // shell_size == place, value, 0.0)
                at = lax.div(shell, per)
                acc_ref[at] = acc_ref[at] + value
        return carry

    lax.fori_loop(0, sources, add, 0)
    step = lanes - depth
    for piece, out_ref in enumerate(outs):
        for spot in range(out_ref.shape[0]):
            flips = (piece >> 1, spot >> 2, (spot >> 1) & 1, spot & 1, piece & 1)
            block = jnp.int32(0)
            for axis, flip in enumerate(flips):
                block = 2 * block + jnp.bitwise_xor(at_ref[axis], flip)
            turn = block * step
            before = pltpu.roll(acc_ref[jnp.maximum(block - 1, 0)], turn, 1)
            after = pltpu.roll(acc_ref[block], turn, 1)
            value = jnp.where(lane < turn, before, after)
            out_ref[spot] = jnp.where(lane < depth, value, 0.0).astype(out_ref.dtype)


def sum_shells(nu, at, got, shell_size, shell_count, depth):
    sources, groups, rows, lanes = got.shape
    tile_count = shell_count // (lanes // shell_size) + 1

    def body(*refs):
        sum_shells_body(*refs, shell_size=shell_size, depth=depth)

    return pl.pallas_call(
        body,
        out_shape=[jax.ShapeDtypeStruct((sources // 4, rows, lanes), jnp.bfloat16)] * 4,
        in_specs=[
            pl.BlockSpec(memory_space=pltpu.SMEM),
            pl.BlockSpec(memory_space=pltpu.SMEM),
            pl.BlockSpec(memory_space=pltpu.VMEM),
        ],
        out_specs=[pl.BlockSpec(memory_space=pltpu.VMEM)] * 4,
        scratch_shapes=[pltpu.VMEM((tile_count, rows, lanes), jnp.float32)],
        compiler_params=pltpu.CompilerParams(vmem_limit_bytes=32 * 1024 * 1024),
        cost_estimate=pl.CostEstimate(flops=10**7, bytes_accessed=4 * 10**6, transcendentals=0),
        name="sum_shells",
    )(nu, at, got)


def transform_body(*refs, part, count, pieces):
    halves, panels = refs[:pieces], refs[pieces : pieces + count]
    outs, gathered = refs[pieces + count : -1], refs[-1]
    unused_dim, rows, lanes = halves[0].shape
    columns = panels[0].shape[1]
    for piece, half_ref in enumerate(halves):
        for block in range(count):
            gathered[piece * rows : (piece + 1) * rows, block * lanes : (block + 1) * lanes] = half_ref[block]
    for start in range(0, columns, part):
        panel = jnp.concatenate([panel_ref[:, start : start + part] for panel_ref in panels], axis=0)
        total = jnp.dot(gathered[...], panel, preferred_element_type=jnp.float32)
        for piece, out_ref in enumerate(outs):
            out_ref[:, start : start + part] = total[piece * rows : (piece + 1) * rows].astype(out_ref.dtype)


def transform(halves, panels, dtypes, part):
    blocks, rows, lanes = halves[0].shape
    depth, columns = panels[0].shape
    pieces = len(halves)

    def body(*refs):
        transform_body(*refs, part=part, count=blocks, pieces=pieces)

    return pl.pallas_call(
        body,
        out_shape=[jax.ShapeDtypeStruct((rows, columns), dtype) for dtype in dtypes],
        in_specs=[pl.BlockSpec(memory_space=pltpu.VMEM)] * (pieces + blocks),
        out_specs=[pl.BlockSpec(memory_space=pltpu.VMEM)] * pieces,
        scratch_shapes=[pltpu.VMEM((pieces * rows, blocks * lanes), jnp.bfloat16)],
        compiler_params=pltpu.CompilerParams(vmem_limit_bytes=24 * 1024 * 1024),
        cost_estimate=pl.CostEstimate(
            flops=2 * pieces * rows * blocks * depth * columns, bytes_accessed=8 * 10**6, transcendentals=0
        ),
        name="second_quarter",
    )(*halves, *panels)


def on_device(tiles, occ_coef, vir_coef, shell_pairs, live_flags):
    slot_count, shell_size, unused_dim, ket_cols = tiles.shape
    basis_count, occ_count = occ_coef.shape
    shell_count = basis_count // shell_size
    depth, vir_count = vir_coef.shape
    device_count = lax.axis_size(AXES)
    device_index = lax.axis_index(AXES)
    ket_owned = ket_cols // device_count
    swap = [(0, 1), (1, 0)]

    filled = jnp.pad(vir_coef, ((0, 2 * shell_size - depth), (0, 0)))
    diagonal = [(i, 3 - i) for i in range(4)]
    by_near = lax.ppermute(filled, NEAR, swap)
    by_row = lax.ppermute(filled, ROW, swap)
    by_col = lax.ppermute(filled, COL, swap)

    flags = live_flags.reshape(device_count, slot_count)
    rank = jnp.cumsum(flags, axis=1) - 1
    chosen = (rank[:, None, :] == jnp.arange(LIVE)[None, :, None]) & (flags[:, None, :] == 1)
    nu_table = shell_pairs[1].reshape(device_count, 1, slot_count)
    nu = jnp.where(jnp.any(chosen, axis=2), jnp.sum(jnp.where(chosen, nu_table, 0), axis=2), shell_count)
    me = jnp.reshape(device_index, (1,)).astype(jnp.int32)
    quarter = first_quarter(me, live_flags, shell_pairs, occ_coef.T, tiles, device_count)
    got = lax.all_to_all(quarter, AXES, split_axis=0, concat_axis=0, tiled=True)
    near_row = lax.ppermute(by_near, ROW, swap)
    near_col = lax.ppermute(by_col, NEAR, swap)
    row_col = lax.ppermute(by_row, COL, swap)

    at = jnp.stack([lax.axis_index(axis) for axis in AXES])
    own, to_core, to_far, to_both = sum_shells(shell_list(nu).reshape(-1), at, got, shell_size, shell_count, depth)
    own, near_row = lax.optimization_barrier((own, near_row))
    all_three = lax.ppermute(near_row, COL, swap)
    panels = [filled, by_col, by_row, row_col, by_near, near_col, near_row, all_three]
    from_far = lax.ppermute(to_far, FAR, swap)
    from_both = lax.ppermute(to_both, (FAR, CORE), diagonal)
    from_core = lax.ppermute(to_core, CORE, swap)
    wide, narrow = jnp.float32, jnp.bfloat16
    own_part, own_peer, far_part, far_peer = transform(
        [own, from_core, from_far, from_both], panels, [wide, narrow, wide, narrow], 512
    )
    far_peer = lax.ppermute(far_peer, CORE, swap)
    far_part = (far_part + far_peer.astype(jnp.float32)).astype(jnp.bfloat16)
    own_peer, far_part = lax.optimization_barrier((own_peer, far_part))
    taken = lax.ppermute(far_part, FAR, swap)
    own_peer = lax.ppermute(own_peer, CORE, swap)
    total = own_part + own_peer.astype(jnp.float32) + taken.astype(jnp.float32)
    return total.reshape(ket_owned, occ_count, vir_count).astype(jnp.bfloat16)


def solution(mesh):
    shape = dict(mesh.shape)
    in_specs = (
        P(("pair", "coef"), None, None, None),
        P("coef", "groups"),
        P("pair", "coef"),
        P(),
        P(),
    )
    out_specs = P("pair", "groups", "coef")
    body = plain
    if shape["pair"] == 32 and shape["coef"] == 1 and shape["groups"] == 1:
        mesh = Mesh(mesh.devices.reshape(2, 2, 2, 2, 2), AXES)
        in_specs = (P(AXES), P(), P(AXES), P(), P())
        out_specs = P(AXES)
        body = on_device
    return jax.shard_map(body, mesh=mesh, in_specs=in_specs, out_specs=out_specs, check_vma=False)
```

```python
import jax
import jax.numpy as jnp
from jax import lax
from jax.experimental import pallas as pl
from jax.experimental.pallas import tpu as pltpu
from jax.sharding import Mesh, PartitionSpec as P

LIVE = 4
FAR, NEAR, ROW, COL, CORE = "far", "near", "row", "col", "core"
AXES = (FAR, NEAR, ROW, COL, CORE)


def plain(tiles, occ_coef, vir_coef, shell_pairs, live_flags):
    slot_count, shell_size, unused_dim, ket_cols = tiles.shape
    pair_count = lax.axis_size("pair")
    coef_count = lax.axis_size("coef")
    core_index = lax.axis_index("coef")
    device_index = lax.axis_index(("pair", "coef"))
    occ_full = lax.all_gather(occ_coef, "coef", axis=0, tiled=True)
    basis_count, occ_count = occ_full.shape
    shell_count = basis_count // shell_size
    ket_owned = ket_cols // pair_count
    occ_shells = occ_full.reshape(shell_count, shell_size, occ_count)
    block_table = shell_pairs.reshape(2, pair_count * coef_count, slot_count)
    flag_table = live_flags.reshape(pair_count * coef_count, slot_count)
    own_mu = lax.dynamic_index_in_dim(block_table[0], device_index, 0, keepdims=False)
    own_flag = lax.dynamic_index_in_dim(flag_table, device_index, 0, keepdims=False)
    peer_nu = lax.dynamic_index_in_dim(
        block_table[1].reshape(pair_count, coef_count, slot_count), core_index, 1, keepdims=False
    )
    panels = jnp.take(occ_shells, own_mu, axis=0)
    result = jnp.einsum("bmi,bmnk->bkin", panels, tiles, preferred_element_type=jnp.float32)
    result = result * own_flag.astype(jnp.float32)[:, None, None, None]
    quarter = result.reshape(tiles.shape[0], ket_cols, occ_count * shell_size)
    received = lax.all_to_all(quarter, "pair", split_axis=1, concat_axis=0, tiled=True)
    recv_shells = peer_nu.reshape(-1)
    selector = (jnp.arange(shell_count, dtype=jnp.int32)[:, None] == recv_shells[None, :]).astype(
        jnp.float32
    )
    received = received.reshape(-1, ket_owned, occ_count, shell_size)
    partial_sum = jnp.einsum("gb,bkis->kigs", selector, received, precision=lax.Precision.HIGHEST)
    half_sum = lax.psum(partial_sum, "coef")
    half_ints = half_sum.reshape(ket_owned * occ_count, basis_count).astype(jnp.bfloat16)
    result = jnp.dot(
        half_ints,
        lax.all_gather(vir_coef, "pair", axis=0, tiled=True),
        preferred_element_type=jnp.float32,
    )
    return result.reshape(ket_owned, occ_count, vir_coef.shape[1]).astype(jnp.bfloat16)


def shell_list_body(nu_ref, out_ref):
    out_ref[...] = nu_ref[...]


def shell_list(nu):
    return pl.pallas_call(
        shell_list_body,
        out_shape=jax.ShapeDtypeStruct(nu.shape, nu.dtype),
        in_specs=[pl.BlockSpec(memory_space=pltpu.VMEM)],
        out_specs=pl.BlockSpec(memory_space=pltpu.VMEM),
        cost_estimate=pl.CostEstimate(flops=10**11, bytes_accessed=10**6, transcendentals=0),
        name="shell_list",
    )(nu)


def first_quarter_body(me_ref, flag_ref, pair_ref, occ_ref, tiles_ref, out_ref, held, turned, wide, sem, *, slots):
    live, shell_size, unused_dim, ket_cols = held.shape
    occ_count = occ_ref.shape[0]
    owners, groups, rows, lanes = out_ref.shape
    step = 16
    first = me_ref[0] * slots
    seen = jnp.int32(0)
    picks = [jnp.int32(0)] * live
    for slot in range(slots):
        flag = flag_ref[first + slot]
        picks = [jnp.where((flag == 1) & (seen == j), slot, pick) for j, pick in enumerate(picks)]
        seen = seen + flag
    copies = [
        pltpu.make_async_copy(tiles_ref.at[pick], held.at[j], sem.at[j]) for j, pick in enumerate(picks)
    ]
    for copy in copies:
        copy.start()
    inner = shell_size * step
    spread = (
        lax.broadcasted_iota(jnp.int32, (shell_size, inner), 1) // step
        == lax.broadcasted_iota(jnp.int32, (shell_size, inner), 0)
    ).astype(jnp.bfloat16)
    diagonal = lax.broadcasted_iota(jnp.int32, (step, inner), 1) % step == lax.broadcasted_iota(
        jnp.int32, (step, inner), 0
    )
    for j in range(live):
        mu = pair_ref[0, first + picks[j]]
        both = occ_ref[:, pl.ds(pl.multiple_of(lax.div(mu, 2) * 128, 128), 128)].astype(jnp.float32)
        both = jnp.where(lax.rem(mu, 2) == 1, pltpu.roll(both, shell_size, 1), both)
        panel = both[:, :shell_size].astype(jnp.bfloat16)
        panel = jnp.dot(panel, spread, preferred_element_type=jnp.float32)
        weight = jnp.where(diagonal[None], panel[:, None, :], 0.0).astype(jnp.bfloat16)
        weight = weight.reshape(occ_count * step, inner)
        copies[j].wait()
        for part in range(0, shell_size // step, 2):
            block = jnp.concatenate(
                [held[j, :, p * step : (p + 1) * step, :].reshape(inner, ket_cols) for p in (part, part + 1)], axis=1
            )
            result = jnp.dot(weight, block, preferred_element_type=jnp.float32)
            for p in range(2):
                at = (part + p) * step
                turned[j % 2, :, at : at + step, :] = result[:, p * ket_cols : (p + 1) * ket_cols].reshape(
                    occ_count, step, ket_cols
                )
        if j % 2 == 1:
            for i in range(occ_count):
                value = turned[:, i].reshape(2 * shell_size, ket_cols)
                wide[pl.ds(i, ket_cols, stride=occ_count), :] = value.T
            out_ref[:, j // 2] = wide[...].astype(jnp.bfloat16).reshape(owners, rows, lanes)


def first_quarter(me, flags, pairs, occ, tiles, owners):
    slots, shell_size, unused_dim, ket_cols = tiles.shape
    occ_count = occ.shape[0]
    rows = ket_cols // owners * occ_count
    shape = (owners, LIVE // 2, rows, 2 * shell_size)

    def body(*refs):
        first_quarter_body(*refs, slots=slots)

    return pl.pallas_call(
        body,
        out_shape=jax.ShapeDtypeStruct(shape, jnp.bfloat16),
        in_specs=[pl.BlockSpec(memory_space=pltpu.SMEM)] * 3
        + [pl.BlockSpec(memory_space=pltpu.VMEM), pl.BlockSpec(memory_space=pl.ANY)],
        out_specs=pl.BlockSpec(memory_space=pltpu.VMEM),
        scratch_shapes=[
            pltpu.VMEM((LIVE, shell_size, shell_size, ket_cols), jnp.bfloat16),
            pltpu.VMEM((2, occ_count, shell_size, ket_cols), jnp.float32),
            pltpu.VMEM((ket_cols * occ_count, 2 * shell_size), jnp.float32),
            pltpu.SemaphoreType.DMA((LIVE,)),
        ],
        compiler_params=pltpu.CompilerParams(vmem_limit_bytes=60 * 1024 * 1024),
        cost_estimate=pl.CostEstimate(flops=10**9, bytes_accessed=6 * 10**6, transcendentals=0),
        name="first_quarter",
    )(me, flags, pairs, occ, tiles)


def sum_shells_body(nu_ref, at_ref, got_ref, *refs, shell_size, depth):
    outs, acc_ref = refs[:-1], refs[-1]
    tile_count, rows, lanes = acc_ref.shape
    per = lanes // shell_size
    sources, groups = got_ref.shape[0], got_ref.shape[1]
    acc_ref[...] = jnp.zeros_like(acc_ref)
    lane = lax.broadcasted_iota(jnp.int32, (rows, lanes), 1)

    def add(source, carry):
        for group in range(groups):
            both = got_ref[source, group].astype(jnp.float32)
            turned = pltpu.roll(both, shell_size, 1)
            for part in range(per):
                shell = nu_ref[source * groups * per + group * per + part]
                place = lax.rem(shell, per)
                value = jnp.where(place == part, both, turned)
                value = jnp.where(lane // shell_size == place, value, 0.0)
                at = lax.div(shell, per)
                acc_ref[at] = acc_ref[at] + value
        return carry

    lax.fori_loop(0, sources, add, 0, unroll=8)
    step = lanes - depth
    for piece, out_ref in enumerate(outs):
        for spot in range(out_ref.shape[0]):
            flips = (piece >> 1, spot >> 2, (spot >> 1) & 1, spot & 1, piece & 1)
            block = jnp.int32(0)
            for axis, flip in enumerate(flips):
                block = 2 * block + jnp.bitwise_xor(at_ref[axis], flip)
            turn = block * step
            before = pltpu.roll(acc_ref[jnp.maximum(block - 1, 0)], turn, 1)
            after = pltpu.roll(acc_ref[block], turn, 1)
            value = jnp.where(lane < turn, before, after)
            out_ref[spot] = jnp.where(lane < depth, value, 0.0).astype(out_ref.dtype)


def sum_shells(nu, at, got, shell_size, shell_count, depth):
    sources, groups, rows, lanes = got.shape
    tile_count = shell_count // (lanes // shell_size) + 1

    def body(*refs):
        sum_shells_body(*refs, shell_size=shell_size, depth=depth)

    return pl.pallas_call(
        body,
        out_shape=[jax.ShapeDtypeStruct((sources // 4, rows, lanes), jnp.bfloat16)] * 4,
        in_specs=[
            pl.BlockSpec(memory_space=pltpu.SMEM),
            pl.BlockSpec(memory_space=pltpu.SMEM),
            pl.BlockSpec(memory_space=pltpu.VMEM),
        ],
        out_specs=[pl.BlockSpec(memory_space=pltpu.VMEM)] * 4,
        scratch_shapes=[pltpu.VMEM((tile_count, rows, lanes), jnp.float32)],
        compiler_params=pltpu.CompilerParams(vmem_limit_bytes=32 * 1024 * 1024),
        cost_estimate=pl.CostEstimate(flops=10**7, bytes_accessed=4 * 10**6, transcendentals=0),
        name="sum_shells",
    )(nu, at, got)


def transform_body(*refs, part, count, pieces):
    halves, panels = refs[:pieces], refs[pieces : pieces + count]
    outs, gathered = refs[pieces + count : -1], refs[-1]
    unused_dim, rows, lanes = halves[0].shape
    columns = panels[0].shape[1]
    for piece, half_ref in enumerate(halves):
        for block in range(count):
            gathered[piece * rows : (piece + 1) * rows, block * lanes : (block + 1) * lanes] = half_ref[block]
    for start in range(0, columns, part):
        panel = jnp.concatenate([panel_ref[:, start : start + part] for panel_ref in panels], axis=0)
        total = jnp.dot(gathered[...], panel, preferred_element_type=jnp.float32)
        for piece, out_ref in enumerate(outs):
            out_ref[:, start : start + part] = total[piece * rows : (piece + 1) * rows].astype(out_ref.dtype)


def transform(halves, panels, dtypes, part):
    blocks, rows, lanes = halves[0].shape
    depth, columns = panels[0].shape
    pieces = len(halves)

    def body(*refs):
        transform_body(*refs, part=part, count=blocks, pieces=pieces)

    return pl.pallas_call(
        body,
        out_shape=[jax.ShapeDtypeStruct((rows, columns), dtype) for dtype in dtypes],
        in_specs=[pl.BlockSpec(memory_space=pltpu.VMEM)] * (pieces + blocks),
        out_specs=[pl.BlockSpec(memory_space=pltpu.VMEM)] * pieces,
        scratch_shapes=[pltpu.VMEM((pieces * rows, blocks * lanes), jnp.bfloat16)],
        compiler_params=pltpu.CompilerParams(vmem_limit_bytes=24 * 1024 * 1024),
        cost_estimate=pl.CostEstimate(
            flops=2 * pieces * rows * blocks * depth * columns, bytes_accessed=8 * 10**6, transcendentals=0
        ),
        name="second_quarter",
    )(*halves, *panels)


def on_device(tiles, occ_coef, vir_coef, shell_pairs, live_flags):
    slot_count, shell_size, unused_dim, ket_cols = tiles.shape
    basis_count, occ_count = occ_coef.shape
    shell_count = basis_count // shell_size
    depth, vir_count = vir_coef.shape
    device_count = lax.axis_size(AXES)
    device_index = lax.axis_index(AXES)
    ket_owned = ket_cols // device_count
    swap = [(0, 1), (1, 0)]

    filled = jnp.pad(vir_coef, ((0, 2 * shell_size - depth), (0, 0)))
    diagonal = [(i, 3 - i) for i in range(4)]
    by_near = lax.ppermute(filled, NEAR, swap)
    by_row = lax.ppermute(filled, ROW, swap)
    by_col = lax.ppermute(filled, COL, swap)

    flags = live_flags.reshape(device_count, slot_count)
    rank = jnp.cumsum(flags, axis=1) - 1
    chosen = (rank[:, None, :] == jnp.arange(LIVE)[None, :, None]) & (flags[:, None, :] == 1)
    nu_table = shell_pairs[1].reshape(device_count, 1, slot_count)
    nu = jnp.where(jnp.any(chosen, axis=2), jnp.sum(jnp.where(chosen, nu_table, 0), axis=2), shell_count)
    me = jnp.reshape(device_index, (1,)).astype(jnp.int32)
    quarter = first_quarter(me, live_flags, shell_pairs, occ_coef.T, tiles, device_count)
    got = lax.all_to_all(quarter, AXES, split_axis=0, concat_axis=0, tiled=True)
    near_row = lax.ppermute(by_near, ROW, swap)
    near_col = lax.ppermute(by_col, NEAR, swap)
    row_col = lax.ppermute(by_row, COL, swap)

    at = jnp.stack([lax.axis_index(axis) for axis in AXES])
    own, to_core, to_far, to_both = sum_shells(shell_list(nu).reshape(-1), at, got, shell_size, shell_count, depth)
    own, near_row = lax.optimization_barrier((own, near_row))
    all_three = lax.ppermute(near_row, COL, swap)
    panels = [filled, by_col, by_row, row_col, by_near, near_col, near_row, all_three]
    from_far = lax.ppermute(to_far, FAR, swap)
    from_both = lax.ppermute(to_both, (FAR, CORE), diagonal)
    from_core = lax.ppermute(to_core, CORE, swap)
    wide, narrow = jnp.float32, jnp.bfloat16
    own_part, own_peer, far_part, far_peer = transform(
        [own, from_core, from_far, from_both], panels, [wide, narrow, wide, narrow], 512
    )
    far_peer = lax.ppermute(far_peer, CORE, swap)
    far_part = (far_part + far_peer.astype(jnp.float32)).astype(jnp.bfloat16)
    own_peer, far_part = lax.optimization_barrier((own_peer, far_part))
    taken = lax.ppermute(far_part, FAR, swap)
    own_peer = lax.ppermute(own_peer, CORE, swap)
    total = own_part + own_peer.astype(jnp.float32) + taken.astype(jnp.float32)
    return total.reshape(ket_owned, occ_count, vir_count).astype(jnp.bfloat16)


def solution(mesh):
    shape = dict(mesh.shape)
    in_specs = (
        P(("pair", "coef"), None, None, None),
        P("coef", "groups"),
        P("pair", "coef"),
        P(),
        P(),
    )
    out_specs = P("pair", "groups", "coef")
    body = plain
    if shape["pair"] == 32 and shape["coef"] == 1 and shape["groups"] == 1:
        mesh = Mesh(mesh.devices.reshape(2, 2, 2, 2, 2), AXES)
        in_specs = (P(AXES), P(), P(AXES), P(), P())
        out_specs = P(AXES)
        body = on_device
    return jax.shard_map(body, mesh=mesh, in_specs=in_specs, out_specs=out_specs, check_vma=False)
```
